32 devices in a mesh: replica: 1, ep: 32 (over z, y, x, core).
Axes of the slice: x: 2, y: 2, z: 4, core: 2. Of those that a mesh axis runs over, the one named last changes fastest.
Arguments:
- tokens: bfloat16 [2, 512, 3584], P(None, ('replica', 'ep')), may hold values from -6 to 6
- routes: int32 [2, 512, 8], P(None, ('replica', 'ep')), may hold values from 0 to 31, all different within a row; in each aligned block of 16 rows (0 to 15, 16 to 31, ..., all dimensions but the last counted through in order) at most 8 rows name the same one
- gates: float32 [2, 512, 8], P(None, ('replica', 'ep')), may hold values from 0.1 to 1
- weights: bfloat16 [32, 3584, 1024], P('ep'), may hold values from -0.09375 to 0.09375
Outputs:
- mixed: bfloat16 [2, 512, 1024], P(None, ('replica', 'ep'))
The draws below stay inside these ranges and needn't reach their ends.
Inputs may be any that keep to these rules, and one draw needn't show every extreme that they name: `routes`: each row names 8 different experts. In each micro-batch the 16 rows of one device name no expert more than 8 times, and in some of these blocks one expert exactly 8 times.
All inputs are finite; a program needn't handle non-finite values.
Results may differ from the reference program's by a relative error of at most 0.0095.
Values may be sent and summed in bfloat16 or wider, within the bound.
A program may use at most 64 MiB of HBM per device.

```python
import math
import jax
import jax.numpy as jnp
import numpy as np
from jax import lax

D_WIN = 3584
FF_WIN = 1024
TOP = 8
MB = 2
TOK_MB = 16
EXPERTS = 32
TOKENS = 512
CAP = 8
GROUPS = 28


def levels(rng, shape, cuts, smallest, high):
    gain = 1.0
    for position, blocks in cuts:
        draws = jax.random.uniform(jax.random.fold_in(jax.random.fold_in(rng, 6), position), (blocks,), jnp.float32, smallest / len(cuts), high / len(cuts))
        gain = gain * jnp.repeat(jnp.exp(draws), shape[position] // blocks).reshape((-1,) + (1,) * (len(shape) - 1 - position))
    return gain


def assign_block(rng, own, number, rows, number_of, top, limit, skew):
    sequence = jax.random.permutation(rng, number_of)
    heavy_load, common = load_shares(number_of, rows * top, limit, skew, True), load_shares(number_of, rows * top, limit, skew, False)
    places = jnp.arange(number_of)

    def named(lengths, rotation):
        used = int((lengths > 0).sum())
        fixed = max(1, used // 4)
        moved = fixed + (places - fixed + rotation * (used - fixed)) % max(1, number_of - fixed)
        return jnp.zeros((number_of,), jnp.int32).at[sequence[jnp.where(places < fixed, places, moved)]].set(jnp.asarray(lengths, jnp.int32))

    lengths = jnp.where(number % 4 == 0, named(heavy_load, number // 4), named(common, number - number // 4 - 1))
    mixed = jax.random.permutation(jax.random.fold_in(own, 3), number_of)
    source_of, sink = mixed[0:number_of // 2 * 2:2], mixed[1:number_of // 2 * 2:2]
    margin = jnp.minimum(lengths[source_of] - 1, limit - lengths[sink]) // 2
    margin = jnp.where((source_of == sequence[0]) | (sink == sequence[0]) | (lengths[sink] == 0), 0, jnp.maximum(margin, 0))
    moved = jax.random.randint(jax.random.fold_in(own, 4), (number_of // 2,), 0, 1 << 20) % (margin + 1)
    lengths = lengths.at[source_of].add(-moved).at[sink].add(moved)
    members = jnp.searchsorted(jnp.cumsum(lengths), jnp.arange(rows * top), side="right").astype(jnp.int32)
    table = members.reshape(top, rows).T
    table = table[jax.random.permutation(jax.random.fold_in(own, 1), rows)]
    rotation = jax.random.randint(jax.random.fold_in(own, 2), (rows, 1), 0, top)
    return jnp.take_along_axis(table, (jnp.arange(top)[None, :] + rotation) % top, axis=1)


def load_shares(count, total, limit, slope, full):
    loads = [(1 << 20) // math.isqrt(grade ** slope) + 1 for grade in range(1, count + 1)]
    largest = limit if full else min(limit, max(-(-total // count), total * loads[0] // sum(loads)))
    least = 1 if total - largest >= count - 1 else 0
    given, spare = [largest] + [least] * (count - 1), total - largest - least * (count - 1)
    while spare > 0:
        movable = [i for i in range(1, count) if given[i] < largest] or [i for i in range(1, count) if given[i] < limit]
        whole, budget = sum([loads[i] for i in movable]), spare
        for i in movable:
            addition = min(limit - given[i], max(1, budget * loads[i] // whole), spare)
            given[i] = given[i] + addition
            spare = spare - addition
    return np.array(given)


def normal_values(rng, extent, deviation, limit, pieces=(), kind=jnp.bfloat16):
    drawn = deviation * jax.random.normal(rng, extent, jnp.float32)
    if pieces:
        drawn = drawn * levels(rng, extent, pieces, -0.22, 0.18)
    return jnp.clip(drawn, -limit, limit).astype(kind)


def setup_inputs(seed: int = 0, part: int = 0) -> dict:
    arg_keys = jax.random.split(jax.random.key(seed), 5)
    own_keys = jax.random.split(jax.random.fold_in(arg_keys[4], part), 5)
    tokens = normal_values(own_keys[0], (MB, TOKENS, D_WIN), 1.0, 6.0, ((1, 32),))
    routes_keys = jax.random.split(jax.random.fold_in(own_keys[1], 1), MB * TOKENS // TOK_MB)
    routes_turns = jax.random.permutation(jax.random.fold_in(own_keys[1], 3), MB * TOKENS // TOK_MB)
    routes = jax.vmap(lambda own, number: assign_block(jax.random.fold_in(own_keys[1], 2), own, number, TOK_MB, EXPERTS, TOP, CAP, 2))(routes_keys, routes_turns).reshape((MB, TOKENS, TOP))
    gates = jnp.clip(0.1 + 0.9 * jax.random.uniform(own_keys[2], (MB, TOKENS, TOP), jnp.float32) ** levels(own_keys[2], (MB, TOKENS, TOP), ((1, 32),), -0.2, 0.2), 0.1, 1.0)
    weights = normal_values(arg_keys[3], (EXPERTS, D_WIN, FF_WIN), D_WIN ** -0.5, 0.09375, ((0, 32),))
    return {"tokens": tokens, "routes": routes, "gates": gates, "weights": weights}


block_rows = 16


def expert_blocks(rows, sorted_ids, weights):
    count = rows.shape[0] // block_rows
    width = weights.shape[2]

    def one(index):
        start = (index * block_rows).astype(jnp.int32)
        part = lax.dynamic_slice_in_dim(rows, start, block_rows, 0)
        part_ids = lax.dynamic_slice_in_dim(sorted_ids, start, block_rows, 0)

        def cond(carry):
            return carry[0] <= part_ids[block_rows - 1]

        def step(carry):
            expert, total = carry
            matrix = lax.dynamic_index_in_dim(weights, expert, 0, keepdims=False)
            hidden = jnp.dot(part, matrix, preferred_element_type=jnp.float32)
            total = jnp.where((part_ids == expert)[:, None], jax.nn.silu(hidden), total)
            return expert + 1, total

        init = (part_ids[0], jnp.zeros((block_rows, width), jnp.float32))
        return lax.while_loop(cond, step, init)[1]

    result = lax.map(one, jnp.arange(count, dtype=jnp.int32))
    return result.reshape(count * block_rows, width).astype(jnp.bfloat16)


def reference(tokens, routes, gates, weights):
    outputs = []
    for micro in range(MB):
        grouped = tokens[micro].astype(jnp.float32).reshape(TOKENS, GROUPS, 128)
        amax = jnp.max(jnp.abs(grouped), axis=2)
        scale = ((amax + 1e-6) / 448.0).astype(jnp.bfloat16)
        factor = scale.astype(jnp.float32)[:, :, None]
        quant = (grouped / factor).astype(jnp.bfloat16)
        restored = (quant.astype(jnp.float32) * factor).astype(jnp.bfloat16).reshape(TOKENS, D_WIN)
        ids = routes[micro].reshape(-1)
        order = jnp.argsort(ids, stable=True).astype(jnp.int32)
        sorted_ids = ids[order]
        token_of = order // TOP
        act = expert_blocks(restored[token_of], sorted_ids, weights)
        weighted = gates[micro].reshape(-1)[order][:, None] * act.astype(jnp.float32)
        total = jnp.zeros((TOKENS, FF_WIN), jnp.float32).at[token_of].add(weighted)
        outputs.append(total.astype(jnp.bfloat16))
    return jnp.stack(outputs)
```

```python
import jax
import jax.numpy as jnp
from jax import lax
from jax.sharding import PartitionSpec as P


def restore(tokens):
    rows, width = tokens.shape
    grouped = tokens.astype(jnp.float32).reshape(rows, width // 128, 128)
    amax = jnp.max(jnp.abs(grouped), axis=2)
    scale = ((amax + 1e-06) / 448.0).astype(jnp.bfloat16).astype(jnp.float32)[:, :, None]
    quant = (grouped / scale).astype(jnp.bfloat16)
    return (quant.astype(jnp.float32) * scale).astype(jnp.bfloat16).reshape(rows, width)


def shards(tokens, routes, gates, weights):
    n_ep = lax.axis_size("ep")
    local = weights.shape[0]
    experts = local * n_ep
    micro, per, width = tokens.shape
    rows = micro * per
    restored = restore(tokens.reshape(rows, width))
    ids = routes.reshape(rows, -1)
    values = gates.reshape(rows, -1)
    names = jnp.arange(experts, dtype=jnp.int32)
    dense = jnp.sum(
        jnp.where(ids[:, :, None] == names[None, None, :], values[:, :, None], 0.0), axis=1
    )
    share = lax.all_to_all(
        dense.reshape(rows, n_ep, local), "ep", split_axis=1, concat_axis=0, tiled=True
    ).reshape(n_ep * rows, local)
    everyone = lax.all_gather(restored, "ep", axis=0, tiled=True)
    total = 0.0
    for j in range(local):
        hidden = jnp.dot(everyone, weights[j], preferred_element_type=jnp.float32)
        act = jax.nn.silu(hidden).astype(jnp.bfloat16).astype(jnp.float32)
        gate = share[:, j : j + 1]
        total = total + jnp.where(gate > 0.0, act, 0.0) * gate
    mixed = lax.psum_scatter(total, "ep", scatter_dimension=0, tiled=True)
    return mixed.astype(jnp.bfloat16).reshape(micro, per, -1)


def solution(mesh):
    placed = (
        P(None, ("replica", "ep"), None),
        P(None, ("replica", "ep"), None),
        P(None, ("replica", "ep"), None),
        P("ep", None, None),
    )
    return jax.shard_map(
        shards,
        mesh=mesh,
        in_specs=placed,
        out_specs=P(None, ("replica", "ep"), None),
        check_vma=False,
    )
```

```python
import functools

import jax
import jax.numpy as jnp
from jax import lax
from jax.experimental import pallas as pl
from jax.experimental.pallas import tpu as pltpu
from jax.sharding import PartitionSpec as P


MESH = pl.DeviceIdType.MESH


def kernel(per, width, ff, experts, tok, routes, gates, w_hbm, out,
           got, w, mine, cs, cr, p1s, p1r, p2s, p2r, tot, zs, zr, fs, fr,
           w_sem, send_sem, got_sem, c_sem, p1_sem, p2_sem, z_sem, f_sem):
    me = lax.axis_index("ep")
    c, x, y, z = me % 2, (me // 2) % 2, (me // 4) % 2, me // 8
    ox, oy, oc = 1 - x, 1 - y, 1 - c
    half = ff // 2
    quarter = 8 * per

    def device(zz, yy, xx, cc):
        return ((zz * 2 + yy) * 2 + xx) * 2 + cc

    def place(yy, xx, h, cc, zz):
        return (((yy * 2 + xx) * 2 + h) * 2 + cc) * 4 + zz

    others = [(z + k) % 4 for k in range(4)]
    earlier = [(z + 4 - k) % 4 for k in range(4)]
    x_dev, y_dev, c_dev = device(z, y, ox, c), device(z, oy, x, c), device(z, y, x, oc)
    z_dev = [device(others[k], y, x, c) for k in range(4)]

    w_copy = pltpu.make_async_copy(w_hbm.at[0], w, w_sem)
    w_copy.start()
    barrier = pltpu.get_barrier_semaphore()
    for dev in (x_dev, y_dev, c_dev, z_dev[1], z_dev[2], z_dev[3]):
        pl.semaphore_signal(barrier, inc=1, device_id={"ep": dev}, device_id_type=MESH)

    lane = lax.broadcasted_iota(jnp.int32, (per, 128), 1)
    for h in range(2):
        rows = pl.ds(pl.multiple_of(place(y, x, h, c, z) * per, per), per)
        for g in range(width // 128):
            v = tok[h, :, g * 128 : (g + 1) * 128].astype(jnp.float32)
            amax = jnp.max(jnp.abs(v), axis=1, keepdims=True)
            scale = ((amax + 1e-06) / 448.0).astype(jnp.bfloat16).astype(jnp.float32)
            quant = (v / scale).astype(jnp.bfloat16).astype(jnp.float32)
            got[rows, g * 128 : (g + 1) * 128] = (quant * scale).astype(jnp.bfloat16)
        names, values = routes[h], gates[h]
        high = jnp.zeros((per, 128), jnp.float32)
        low = jnp.zeros((per, 128), jnp.float32)
        for k in range(names.shape[1]):
            name, value = names[:, k : k + 1], values[:, k : k + 1]
            high = high + jnp.where(lane == name, value, 0.0)
            low = low + jnp.where(lane - experts == name, value, 0.0)
        low = low - low.astype(jnp.bfloat16).astype(jnp.float32)
        got[rows, width : width + 128] = jnp.where(lane < experts, high, low).astype(jnp.bfloat16)

    pl.semaphore_wait(barrier, 6)

    copies = []

    def send(src, dst, sem, dev):
        copy = pltpu.make_async_remote_copy(
            src_ref=src, dst_ref=dst, send_sem=send_sem.at[len(copies)], recv_sem=sem,
            device_id={"ep": dev}, device_id_type=MESH,
        )
        copy.start()
        copies.append(copy)

    def landed(dst, sem):
        pltpu.make_async_remote_copy(
            src_ref=dst, dst_ref=dst, send_sem=send_sem.at[0], recv_sem=sem,
            device_id={"ep": c_dev}, device_id_type=MESH,
        ).wait_recv()

    def block(spot):
        return got.at[pl.ds(pl.multiple_of(spot * per, per), per)]

    def pass_on(spot, devs):
        for dev in devs:
            send(block(spot), block(spot), got_sem.at[spot], dev)

    def arrive(spot):
        landed(block(spot), got_sem.at[spot])

    def sibling_line(yy, xx):
        for h in range(2):
            for k in range(4):
                arrive(place(yy, xx, h, oc, earlier[k]))

    def compute(u, yy, xx):
        base = place(yy, xx, 0, 0, 0) * per
        rows = pl.ds(pl.multiple_of(base, 2 * quarter), 2 * quarter)
        wide = lax.broadcasted_iota(jnp.int32, (2 * quarter, 128), 1)
        share = got[rows, width : width + 128].astype(jnp.float32)
        picked = (wide == me) | (wide == me + experts)
        gate = jnp.sum(jnp.where(picked, share, 0.0), axis=1, keepdims=True)

        def tile(col):
            cols = pl.ds(pl.multiple_of(col, 256), 256)
            v = jnp.dot(got[rows, :width], w[:, cols], preferred_element_type=jnp.float32)
            return gate * (v / (1.0 + jnp.exp(-v)))

        for j in range(half // 256):
            cs[u, :, j * 256 : (j + 1) * 256] = tile(oc * half + j * 256).astype(jnp.bfloat16)
        send(cs.at[u], cr.at[u], c_sem.at[u], c_dev)
        for j in range(half // 256):
            mine[u, :, j * 256 : (j + 1) * 256] = tile(c * half + j * 256)

    for h in range(2):
        pass_on(place(y, x, h, c, z), [x_dev, y_dev, z_dev[1], z_dev[2], z_dev[3], c_dev])
    for k in range(1, 4):
        for h in range(2):
            spot = place(y, x, h, c, earlier[k])
            arrive(spot)
            pass_on(spot, [x_dev, y_dev, c_dev])

    def neighbours(k):
        spot = place(y, ox, 0, c, earlier[k])
        arrive(spot)
        pass_on(spot, [y_dev, c_dev])
        spot = place(oy, x, 1, c, earlier[k])
        arrive(spot)
        pass_on(spot, [x_dev, c_dev])
        spot = place(y, ox, 1, c, earlier[k])
        arrive(spot)
        pass_on(spot, [c_dev])
        spot = place(oy, x, 0, c, earlier[k])
        arrive(spot)
        pass_on(spot, [c_dev])

    neighbours(0)
    w_copy.wait()
    sibling_line(y, x)
    compute(0, y, x)
    for k in range(1, 4):
        neighbours(k)
    sibling_line(y, ox)
    compute(1, y, ox)
    sibling_line(oy, x)
    compute(2, oy, x)

    lo, hi = pl.ds(0, quarter), pl.ds(quarter, quarter)

    def joined(u, rows):
        return mine[u, rows] + cr[u, rows].astype(jnp.float32)

    def first(i, u, rows, dev):
        p1s[i] = joined(u, rows).astype(jnp.bfloat16)
        send(p1s.at[i], p1r.at[i], p1_sem.at[i], dev)

    for k in range(4):
        for h in range(2):
            spot = place(oy, ox, h, c, earlier[k])
            arrive(spot)
            pass_on(spot, [c_dev])
    for u in range(3):
        landed(cr.at[u], c_sem.at[u])
    first(0, 2, lo, y_dev)
    first(1, 1, hi, x_dev)
    sibling_line(oy, ox)
    compute(3, oy, ox)
    landed(cr.at[3], c_sem.at[3])
    first(2, 3, lo, y_dev)
    first(3, 3, hi, x_dev)

    landed(p1r.at[2], p1_sem.at[2])
    p2s[0] = (joined(1, lo) + p1r[2].astype(jnp.float32)).astype(jnp.bfloat16)
    send(p2s.at[0], p2r.at[0], p2_sem.at[0], x_dev)
    landed(p1r.at[3], p1_sem.at[3])
    p2s[1] = (joined(2, hi) + p1r[3].astype(jnp.float32)).astype(jnp.bfloat16)
    send(p2s.at[1], p2r.at[1], p2_sem.at[1], y_dev)
    landed(p1r.at[0], p1_sem.at[0])
    tot[lo] = joined(0, lo) + p1r[0].astype(jnp.float32)
    landed(p1r.at[1], p1_sem.at[1])
    tot[hi] = joined(0, hi) + p1r[1].astype(jnp.float32)
    landed(p2r.at[0], p2_sem.at[0])
    tot[lo] = tot[lo] + p2r[0].astype(jnp.float32)
    landed(p2r.at[1], p2_sem.at[1])
    tot[hi] = tot[hi] + p2r[1].astype(jnp.float32)

    def part(h, cc, zz):
        return tot[pl.ds(pl.multiple_of(((h * 2 + cc) * 4 + zz) * per, per), per)]

    for k in range(1, 4):
        for h in range(2):
            for cc in range(2):
                at = (h * 2 + cc) * per
                zs[k, at : at + per] = part(h, cc, others[k]).astype(jnp.bfloat16)
        send(zs.at[k], zr.at[k], z_sem.at[k], z_dev[k])
    for k in range(1, 4):
        landed(zr.at[k], z_sem.at[k])

    def final(h, cc):
        total = part(h, cc, z)
        for k in range(1, 4):
            rows = pl.ds(pl.multiple_of((h * 2 + cc) * per, per), per)
            total = total + zr[k, rows].astype(jnp.float32)
        return total.astype(jnp.bfloat16)

    for h in range(2):
        fs[h] = final(h, oc)
    send(fs, fr, f_sem, c_dev)
    for h in range(2):
        out[h, :, pl.ds(pl.multiple_of(c * half, half), half)] = final(h, c)
    landed(fr, f_sem)
    for h in range(2):
        out[h, :, pl.ds(pl.multiple_of(oc * half, half), half)] = fr[h]
    for copy in copies:
        copy.wait_send()


def fused(tokens, routes, gates, weights):
    n_ep = lax.axis_size("ep")
    micro, per, width = tokens.shape
    ff = weights.shape[2]
    half, quarter = ff // 2, 8 * per
    bf, f32 = jnp.bfloat16, jnp.float32
    vmem = pl.BlockSpec(memory_space=pltpu.VMEM)
    return pl.pallas_call(
        functools.partial(kernel, per, width, ff, n_ep),
        out_shape=jax.ShapeDtypeStruct((micro, per, ff), bf),
        in_specs=[vmem, vmem, vmem, pl.BlockSpec(memory_space=pl.ANY)],
        out_specs=vmem,
        scratch_shapes=[
            pltpu.VMEM((n_ep * 2 * per, width + 128), bf),
            pltpu.VMEM((width, ff), bf),
            pltpu.VMEM((4, 2 * quarter, half), f32),
            pltpu.VMEM((4, 2 * quarter, half), bf),
            pltpu.VMEM((4, 2 * quarter, half), bf),
            pltpu.VMEM((4, quarter, half), bf),
            pltpu.VMEM((4, quarter, half), bf),
            pltpu.VMEM((2, quarter, half), bf),
            pltpu.VMEM((2, quarter, half), bf),
            pltpu.VMEM((2 * quarter, half), f32),
            pltpu.VMEM((4, 4 * per, half), bf),
            pltpu.VMEM((4, 4 * per, half), bf),
            pltpu.VMEM((2, per, half), bf),
            pltpu.VMEM((2, per, half), bf),
            pltpu.SemaphoreType.DMA,
            pltpu.SemaphoreType.DMA((96,)),
            pltpu.SemaphoreType.DMA((64,)),
            pltpu.SemaphoreType.DMA((4,)),
            pltpu.SemaphoreType.DMA((4,)),
            pltpu.SemaphoreType.DMA((2,)),
            pltpu.SemaphoreType.DMA((4,)),
            pltpu.SemaphoreType.DMA,
        ],
        compiler_params=pltpu.CompilerParams(
            collective_id=0, has_side_effects=True, vmem_limit_bytes=48 * 1024 * 1024
        ),
        cost_estimate=pl.CostEstimate(
            flops=2 * n_ep * 2 * per * width * ff,
            bytes_accessed=2 * width * ff,
            transcendentals=n_ep * 2 * per * ff,
        ),
    )(tokens, routes, gates, weights)


def restore(tokens):
    rows, width = tokens.shape
    grouped = tokens.astype(jnp.float32).reshape(rows, width // 128, 128)
    amax = jnp.max(jnp.abs(grouped), axis=2)
    scale = ((amax + 1e-06) / 448.0).astype(jnp.bfloat16).astype(jnp.float32)[:, :, None]
    quant = (grouped / scale).astype(jnp.bfloat16)
    return (quant.astype(jnp.float32) * scale).astype(jnp.bfloat16).reshape(rows, width)


def shards(tokens, routes, gates, weights):
    n_ep = lax.axis_size("ep")
    local = weights.shape[0]
    experts = local * n_ep
    micro, per, width = tokens.shape
    rows = micro * per
    restored = restore(tokens.reshape(rows, width))
    ids = routes.reshape(rows, -1)
    values = gates.reshape(rows, -1)
    names = jnp.arange(experts, dtype=jnp.int32)
    dense = jnp.sum(
        jnp.where(ids[:, :, None] == names[None, None, :], values[:, :, None], 0.0), axis=1
    )
    share = lax.all_to_all(
        dense.reshape(rows, n_ep, local), "ep", split_axis=1, concat_axis=0, tiled=True
    ).reshape(n_ep * rows, local)
    everyone = lax.all_gather(restored, "ep", axis=0, tiled=True)
    total = 0.0
    for j in range(local):
        hidden = jnp.dot(everyone, weights[j], preferred_element_type=jnp.float32)
        act = jax.nn.silu(hidden).astype(jnp.bfloat16).astype(jnp.float32)
        gate = share[:, j : j + 1]
        total = total + jnp.where(gate > 0.0, act, 0.0) * gate
    mixed = lax.psum_scatter(total, "ep", scatter_dimension=0, tiled=True)
    return mixed.astype(jnp.bfloat16).reshape(micro, per, -1)


def solution(mesh):
    placed = (
        P(None, ("replica", "ep"), None),
        P(None, ("replica", "ep"), None),
        P(None, ("replica", "ep"), None),
        P("ep", None, None),
    )
    small = mesh.shape["ep"] == 32 and mesh.shape["replica"] == 1
    return jax.shard_map(
        fused if small else shards,
        mesh=mesh,
        in_specs=placed,
        out_specs=P(None, ("replica", "ep"), None),
        check_vma=False,
    )
```

```python
import functools

import jax
import jax.numpy as jnp
from jax import lax
from jax.experimental import pallas as pl
from jax.experimental.pallas import tpu as pltpu
from jax.sharding import PartitionSpec as P


MESH = pl.DeviceIdType.MESH


def kernel(per, width, ff, experts, tok, routes, gates, w_hbm, out,
           got, w, mine, cs, cr, p1s, p1r, p2s, p2r, tot, zs, zr, fs, fr,
           w_sem, send_sem, got_sem, c_sem, p1_sem, p2_sem, z_sem, f_sem):
    me = lax.axis_index("ep")
    c, x, y, z = me % 2, (me // 2) % 2, (me // 4) % 2, me // 8
    ox, oy, oc = 1 - x, 1 - y, 1 - c
    half = ff // 2
    quarter = 8 * per
    parts = half // 256

    def device(zz, yy, xx, cc):
        return ((zz * 2 + yy) * 2 + xx) * 2 + cc

    def place(yy, xx, h, cc, zz):
        return (((yy * 2 + xx) * 2 + h) * 2 + cc) * 4 + zz

    others = [(z + k) % 4 for k in range(4)]
    far = z // 2
    line = [z, z + 1 - 2 * (z % 2), 2 - far, 3 - 3 * far]
    inner = (z == 1) | (z == 2)
    x_dev, y_dev, c_dev = device(z, y, ox, c), device(z, oy, x, c), device(z, y, x, oc)
    z_dev = [device(others[k], y, x, c) for k in range(4)]

    w_copy = pltpu.make_async_copy(w_hbm.at[0], w, w_sem)
    w_copy.start()
    barrier = pltpu.get_barrier_semaphore()
    for dev in (x_dev, y_dev, c_dev, z_dev[1], z_dev[2], z_dev[3]):
        pl.semaphore_signal(barrier, inc=1, device_id={"ep": dev}, device_id_type=MESH)

    lane = lax.broadcasted_iota(jnp.int32, (per, 128), 1)
    for h in range(2):
        rows = pl.ds(pl.multiple_of(place(y, x, h, c, z) * per, per), per)
        for g in range(width // 128):
            v = tok[h, :, g * 128 : (g + 1) * 128].astype(jnp.float32)
            amax = jnp.max(jnp.abs(v), axis=1, keepdims=True)
            scale = ((amax + 1e-06) / 448.0).astype(jnp.bfloat16).astype(jnp.float32)
            quant = (v / scale).astype(jnp.bfloat16).astype(jnp.float32)
            got[rows, g * 128 : (g + 1) * 128] = (quant * scale).astype(jnp.bfloat16)
        names, values = routes[h], gates[h]
        high = jnp.zeros((per, 128), jnp.float32)
        low = jnp.zeros((per, 128), jnp.float32)
        for k in range(names.shape[1]):
            name, value = names[:, k : k + 1], values[:, k : k + 1]
            high = high + jnp.where(lane == name, value, 0.0)
            low = low + jnp.where(lane - experts == name, value, 0.0)
        low = low - low.astype(jnp.bfloat16).astype(jnp.float32)
        got[rows, width : width + 128] = jnp.where(lane < experts, high, low).astype(jnp.bfloat16)

    pl.semaphore_wait(barrier, 6)

    copies, inner_copies = [], []

    def prepare(src, dst, sem, dev):
        return pltpu.make_async_remote_copy(
            src_ref=src, dst_ref=dst, send_sem=send_sem.at[len(copies) + len(inner_copies)],
            recv_sem=sem, device_id={"ep": dev}, device_id_type=MESH,
        )

    def send(src, dst, sem, dev):
        copy = prepare(src, dst, sem, dev)
        copy.start()
        copies.append(copy)

    def inner_on(spot, dev):
        copy = prepare(block(spot), block(spot), got_sem.at[spot], dev)
        inner_copies.append(copy)

        @pl.when(inner)
        def _():
            copy.start()

    def landed(dst, sem):
        pltpu.make_async_remote_copy(
            src_ref=dst, dst_ref=dst, send_sem=send_sem.at[0], recv_sem=sem,
            device_id={"ep": c_dev}, device_id_type=MESH,
        ).wait_recv()

    def block(spot):
        return got.at[pl.ds(pl.multiple_of(spot * per, per), per)]

    def pass_on(spot, devs):
        for dev in devs:
            send(block(spot), block(spot), got_sem.at[spot], dev)

    def arrive(spot):
        landed(block(spot), got_sem.at[spot])

    def sibling_line(yy, xx):
        for h in range(2):
            for k in range(4):
                arrive(place(yy, xx, h, oc, line[k]))

    def compute(u, yy, xx):
        base = place(yy, xx, 0, 0, 0) * per
        rows = pl.ds(pl.multiple_of(base, 2 * quarter), 2 * quarter)
        wide = lax.broadcasted_iota(jnp.int32, (2 * quarter, 128), 1)
        share = got[rows, width : width + 128].astype(jnp.float32)
        picked = (wide == me) | (wide == me + experts)
        gate = jnp.sum(jnp.where(picked, share, 0.0), axis=1, keepdims=True)

        def tile(col):
            cols = pl.ds(pl.multiple_of(col, 256), 256)
            v = jnp.dot(got[rows, :width], w[:, cols], preferred_element_type=jnp.float32)
            return gate * (v / (1.0 + jnp.exp(-v)))

        for j in range(parts):
            cs[u, j] = tile(oc * half + j * 256).astype(jnp.bfloat16)
            if u == 3:
                send(cs.at[u, j], cr.at[u, j], c_sem.at[u + j], c_dev)
                mine[u, j] = tile(c * half + j * 256)
                if j > 0:
                    start(j - 1)
        if u < 3:
            send(cs.at[u], cr.at[u], c_sem.at[u], c_dev)
            for j in range(parts):
                mine[u, j] = tile(c * half + j * 256)

    def neighbours(k):
        if k != 1:
            spot = place(y, ox, 0, c, line[k])
            arrive(spot)
            pass_on(spot, [y_dev, c_dev])
            spot = place(oy, x, 1, c, line[k])
            arrive(spot)
            pass_on(spot, [x_dev, c_dev])
        spot = place(y, ox, 1, c, line[k])
        arrive(spot)
        pass_on(spot, [c_dev])
        spot = place(oy, x, 0, c, line[k])
        arrive(spot)
        pass_on(spot, [c_dev])

    def diagonal(k):
        for h in range(2):
            spot = place(oy, ox, h, c, line[k])
            arrive(spot)
            pass_on(spot, [near, c_dev] if k == 0 else [c_dev])

    near, across = device(line[1], y, x, c), device(3 - z, y, x, c)
    for h in range(2):
        spot = place(y, x, h, c, z)
        pass_on(spot, [near])
        inner_on(spot, across)
        pass_on(spot, [x_dev, y_dev, c_dev])
    for k in range(1, 4):
        for h in range(2):
            spot = place(y, x, h, c, line[k])
            arrive(spot)
            inner_on(spot, across if k == 1 else near)
            pass_on(spot, [x_dev, y_dev, c_dev] if k > 1 else [(y_dev, x_dev)[h], c_dev])
        neighbours(k - 1)
    pass_on(place(y, ox, 0, c, z), [near])
    pass_on(place(oy, x, 1, c, z), [near])
    diagonal(0)
    w_copy.wait()
    sibling_line(y, x)
    compute(0, y, x)
    neighbours(3)
    for spot in (place(y, ox, 0, c, line[1]), place(oy, x, 1, c, line[1])):
        arrive(spot)
        pass_on(spot, [c_dev])
    sibling_line(y, ox)
    compute(1, y, ox)
    diagonal(2)
    sibling_line(oy, x)
    compute(2, oy, x)
    diagonal(1)
    diagonal(3)

    lo, hi = pl.ds(0, quarter), pl.ds(quarter, quarter)

    def joined(u, j, rows):
        return mine[u, j, rows] + cr[u, j, rows].astype(jnp.float32)

    def first(i, j, u, rows, dev):
        p1s[i, j] = joined(u, j, rows).astype(jnp.bfloat16)
        send(p1s.at[i, j], p1r.at[i, j], p1_sem.at[i * parts + j], dev)

    def start(j):
        landed(cr.at[3, j], c_sem.at[3 + j])
        first(2, j, 3, lo, y_dev)
        first(3, j, 3, hi, x_dev)

    for u in range(3):
        landed(cr.at[u], c_sem.at[u])
    for j in range(parts):
        first(0, j, 2, lo, y_dev)
        first(1, j, 1, hi, x_dev)
    sibling_line(oy, ox)
    compute(3, oy, ox)
    start(parts - 1)

    for j in range(parts):
        for i, u, rows, dev in ((0, 1, lo, x_dev), (1, 2, hi, y_dev)):
            landed(p1r.at[2 + i, j], p1_sem.at[(2 + i) * parts + j])
            p2s[i, j] = (joined(u, j, rows) + p1r[2 + i, j].astype(jnp.float32)).astype(jnp.bfloat16)
            send(p2s.at[i, j], p2r.at[i, j], p2_sem.at[i * parts + j], dev)
    for j in range(parts):
        for i, rows in ((0, lo), (1, hi)):
            landed(p1r.at[i, j], p1_sem.at[i * parts + j])
            tot[j, rows] = joined(0, j, rows) + p1r[i, j].astype(jnp.float32)

    def part(j, h, cc, zz):
        return tot[j, pl.ds(pl.multiple_of(((h * 2 + cc) * 4 + zz) * per, per), per)]

    for j in range(parts):
        for i, rows in ((0, lo), (1, hi)):
            landed(p2r.at[i, j], p2_sem.at[i * parts + j])
            tot[j, rows] = tot[j, rows] + p2r[i, j].astype(jnp.float32)
        for k in range(1, 4):
            for h in range(2):
                for cc in range(2):
                    at = (h * 2 + cc) * per
                    zs[k, j, at : at + per] = part(j, h, cc, others[k]).astype(jnp.bfloat16)
            send(zs.at[k, j], zr.at[k, j], z_sem.at[k * parts + j], z_dev[k])

    def final(j, h, cc):
        total = part(j, h, cc, z)
        rows = pl.ds(pl.multiple_of((h * 2 + cc) * per, per), per)
        for k in range(1, 4):
            total = total + zr[k, j, rows].astype(jnp.float32)
        return total.astype(jnp.bfloat16)

    for j in range(parts):
        for k in range(1, 4):
            landed(zr.at[k, j], z_sem.at[k * parts + j])
        for h in range(2):
            fs[j, h] = final(j, h, oc)
        send(fs.at[j], fr.at[j], f_sem.at[j], c_dev)
        for h in range(2):
            out[h, :, pl.ds(pl.multiple_of(c * half + j * 256, 256), 256)] = final(j, h, c)
    for j in range(parts):
        landed(fr.at[j], f_sem.at[j])
        for h in range(2):
            out[h, :, pl.ds(pl.multiple_of(oc * half + j * 256, 256), 256)] = fr[j, h]
    for copy in copies:
        copy.wait_send()

    @pl.when(inner)
    def _():
        for copy in inner_copies:
            copy.wait_send()


def fused(tokens, routes, gates, weights):
    n_ep = lax.axis_size("ep")
    micro, per, width = tokens.shape
    ff = weights.shape[2]
    half, quarter = ff // 2, 8 * per
    parts = half // 256
    bf, f32 = jnp.bfloat16, jnp.float32
    vmem = pl.BlockSpec(memory_space=pltpu.VMEM)
    return pl.pallas_call(
        functools.partial(kernel, per, width, ff, n_ep),
        out_shape=jax.ShapeDtypeStruct((micro, per, ff), bf),
        in_specs=[vmem, vmem, vmem, pl.BlockSpec(memory_space=pl.ANY)],
        out_specs=vmem,
        scratch_shapes=[
            pltpu.VMEM((n_ep * 2 * per, width + 128), bf),
            pltpu.VMEM((width, ff), bf),
            pltpu.VMEM((4, parts, 2 * quarter, 256), f32),
            pltpu.VMEM((4, parts, 2 * quarter, 256), bf),
            pltpu.VMEM((4, parts, 2 * quarter, 256), bf),
            pltpu.VMEM((4, parts, quarter, 256), bf),
            pltpu.VMEM((4, parts, quarter, 256), bf),
            pltpu.VMEM((2, parts, quarter, 256), bf),
            pltpu.VMEM((2, parts, quarter, 256), bf),
            pltpu.VMEM((parts, 2 * quarter, 256), f32),
            pltpu.VMEM((4, parts, 4 * per, 256), bf),
            pltpu.VMEM((4, parts, 4 * per, 256), bf),
            pltpu.VMEM((parts, 2, per, 256), bf),
            pltpu.VMEM((parts, 2, per, 256), bf),
            pltpu.SemaphoreType.DMA,
            pltpu.SemaphoreType.DMA((112,)),
            pltpu.SemaphoreType.DMA((64,)),
            pltpu.SemaphoreType.DMA((3 + parts,)),
            pltpu.SemaphoreType.DMA((4 * parts,)),
            pltpu.SemaphoreType.DMA((2 * parts,)),
            pltpu.SemaphoreType.DMA((4 * parts,)),
            pltpu.SemaphoreType.DMA((parts,)),
        ],
        compiler_params=pltpu.CompilerParams(
            collective_id=0, has_side_effects=True, vmem_limit_bytes=48 * 1024 * 1024
        ),
        cost_estimate=pl.CostEstimate(
            flops=2 * n_ep * 2 * per * width * ff,
            bytes_accessed=2 * width * ff,
            transcendentals=n_ep * 2 * per * ff,
        ),
    )(tokens, routes, gates, weights)


def restore(tokens):
    rows, width = tokens.shape
    grouped = tokens.astype(jnp.float32).reshape(rows, width // 128, 128)
    amax = jnp.max(jnp.abs(grouped), axis=2)
    scale = ((amax + 1e-06) / 448.0).astype(jnp.bfloat16).astype(jnp.float32)[:, :, None]
    quant = (grouped / scale).astype(jnp.bfloat16)
    return (quant.astype(jnp.float32) * scale).astype(jnp.bfloat16).reshape(rows, width)


def shards(tokens, routes, gates, weights):
    n_ep = lax.axis_size("ep")
    local = weights.shape[0]
    experts = local * n_ep
    micro, per, width = tokens.shape
    rows = micro * per
    restored = restore(tokens.reshape(rows, width))
    ids = routes.reshape(rows, -1)
    values = gates.reshape(rows, -1)
    names = jnp.arange(experts, dtype=jnp.int32)
    dense = jnp.sum(
        jnp.where(ids[:, :, None] == names[None, None, :], values[:, :, None], 0.0), axis=1
    )
    share = lax.all_to_all(
        dense.reshape(rows, n_ep, local), "ep", split_axis=1, concat_axis=0, tiled=True
    ).reshape(n_ep * rows, local)
    everyone = lax.all_gather(restored, "ep", axis=0, tiled=True)
    total = 0.0
    for j in range(local):
        hidden = jnp.dot(everyone, weights[j], preferred_element_type=jnp.float32)
        act = jax.nn.silu(hidden).astype(jnp.bfloat16).astype(jnp.float32)
        gate = share[:, j : j + 1]
        total = total + jnp.where(gate > 0.0, act, 0.0) * gate
    mixed = lax.psum_scatter(total, "ep", scatter_dimension=0, tiled=True)
    return mixed.astype(jnp.bfloat16).reshape(micro, per, -1)


def solution(mesh):
    placed = (
        P(None, ("replica", "ep"), None),
        P(None, ("replica", "ep"), None),
        P(None, ("replica", "ep"), None),
        P("ep", None, None),
    )
    small = mesh.shape["ep"] == 32 and mesh.shape["replica"] == 1
    return jax.shard_map(
        fused if small else shards,
        mesh=mesh,
        in_specs=placed,
        out_specs=P(None, ("replica", "ep"), None),
        check_vma=False,
    )
```

```python
import functools

import jax
import jax.numpy as jnp
from jax import lax
from jax.experimental import pallas as pl
from jax.experimental.pallas import tpu as pltpu
from jax.sharding import PartitionSpec as P


MESH = pl.DeviceIdType.MESH


def kernel(per, width, ff, experts, tok, routes, gates, w_hbm, out,
           got, w, mine, cs, cr, p1s, p1r, p2s, p2r, tot, zs, zr, fs, fr,
           w_sem, send_sem, got_sem, c_sem, p1_sem, p2_sem, z_sem, f_sem):
    me = lax.axis_index("ep")
    c, x, y, z = me % 2, (me // 2) % 2, (me // 4) % 2, me // 8
    ox, oy, oc = 1 - x, 1 - y, 1 - c
    half = ff // 2
    quarter = 8 * per
    parts = half // 256

    def device(zz, yy, xx, cc):
        return ((zz * 2 + yy) * 2 + xx) * 2 + cc

    def place(yy, xx, h, cc, zz):
        return (((yy * 2 + xx) * 2 + h) * 2 + cc) * 4 + zz

    others = [(z + k) % 4 for k in range(4)]
    far = z // 2
    line = [z, z + 1 - 2 * (z % 2), 2 - far, 3 - 3 * far]
    inner = (z == 1) | (z == 2)
    x_dev, y_dev, c_dev = device(z, y, ox, c), device(z, oy, x, c), device(z, y, x, oc)
    z_dev = [device(others[k], y, x, c) for k in range(4)]

    w_copy = pltpu.make_async_copy(w_hbm.at[0], w, w_sem)
    w_copy.start()
    barrier = pltpu.get_barrier_semaphore()
    for dev in (x_dev, y_dev, c_dev, z_dev[1], z_dev[2], z_dev[3]):
        pl.semaphore_signal(barrier, inc=1, device_id={"ep": dev}, device_id_type=MESH)

    lane = lax.broadcasted_iota(jnp.int32, (per, 128), 1)

    def stage(h):
        rows = pl.ds(pl.multiple_of(place(y, x, h, c, z) * per, per), per)
        for g in range(width // 128):
            v = tok[h, :, g * 128 : (g + 1) * 128].astype(jnp.float32)
            amax = jnp.max(jnp.abs(v), axis=1, keepdims=True)
            scale = ((amax + 1e-06) / 448.0).astype(jnp.bfloat16).astype(jnp.float32)
            quant = (v / scale).astype(jnp.bfloat16).astype(jnp.float32)
            got[rows, g * 128 : (g + 1) * 128] = (quant * scale).astype(jnp.bfloat16)
        names, values = routes[h], gates[h]
        high = jnp.zeros((per, 128), jnp.float32)
        low = jnp.zeros((per, 128), jnp.float32)
        for k in range(names.shape[1]):
            name, value = names[:, k : k + 1], values[:, k : k + 1]
            high = high + jnp.where(lane == name, value, 0.0)
            low = low + jnp.where(lane - experts == name, value, 0.0)
        low = low - low.astype(jnp.bfloat16).astype(jnp.float32)
        got[rows, width : width + 128] = jnp.where(lane < experts, high, low).astype(jnp.bfloat16)

    stage(0)
    pl.semaphore_wait(barrier, 6)

    copies, inner_copies = [], []

    def prepare(src, dst, sem, dev):
        return pltpu.make_async_remote_copy(
            src_ref=src, dst_ref=dst, send_sem=send_sem.at[len(copies) + len(inner_copies)],
            recv_sem=sem, device_id={"ep": dev}, device_id_type=MESH,
        )

    def send(src, dst, sem, dev):
        copy = prepare(src, dst, sem, dev)
        copy.start()
        copies.append(copy)

    def inner_on(spot, dev):
        copy = prepare(block(spot), block(spot), got_sem.at[spot], dev)
        inner_copies.append(copy)

        @pl.when(inner)
        def _():
            copy.start()

    def landed(dst, sem):
        pltpu.make_async_remote_copy(
            src_ref=dst, dst_ref=dst, send_sem=send_sem.at[0], recv_sem=sem,
            device_id={"ep": c_dev}, device_id_type=MESH,
        ).wait_recv()

    def block(spot):
        return got.at[pl.ds(pl.multiple_of(spot * per, per), per)]

    def pass_on(spot, devs):
        for dev in devs:
            send(block(spot), block(spot), got_sem.at[spot], dev)

    def arrive(spot):
        landed(block(spot), got_sem.at[spot])

    def sibling_line(yy, xx):
        for h in range(2):
            for k in range(4):
                arrive(place(yy, xx, h, oc, line[k]))

    def compute(u, yy, xx):
        base = place(yy, xx, 0, 0, 0) * per
        rows = pl.ds(pl.multiple_of(base, 2 * quarter), 2 * quarter)
        wide = lax.broadcasted_iota(jnp.int32, (2 * quarter, 128), 1)
        share = got[rows, width : width + 128].astype(jnp.float32)
        picked = (wide == me) | (wide == me + experts)
        gate = jnp.sum(jnp.where(picked, share, 0.0), axis=1, keepdims=True)

        def tile(col):
            cols = pl.ds(pl.multiple_of(col, 256), 256)
            v = jnp.dot(got[rows, :width], w[:, cols], preferred_element_type=jnp.float32)
            return (gate * (0.5 * v)) * (1.0 + jnp.tanh(0.5 * v))

        for j in range(parts):
            cs[u, j] = tile(oc * half + j * 256).astype(jnp.bfloat16)
            if u == 3:
                send(cs.at[u, j], cr.at[u, j], c_sem.at[u + j], c_dev)
                mine[u, j] = tile(c * half + j * 256)
                if j > 0:
                    start(j - 1)
        if u < 3:
            send(cs.at[u], cr.at[u], c_sem.at[u], c_dev)
            for j in range(parts):
                mine[u, j] = tile(c * half + j * 256)

    def neighbours(k):
        spot = place(y, ox, 0, c, line[k])
        arrive(spot)
        pass_on(spot, [c_dev] if k == 1 else [y_dev, c_dev])
        spot = place(oy, x, 1, c, line[k])
        arrive(spot)
        pass_on(spot, [c_dev] if k == 1 else [x_dev, c_dev])
        spot = place(y, ox, 1, c, line[k])
        arrive(spot)
        pass_on(spot, [c_dev])
        spot = place(oy, x, 0, c, line[k])
        arrive(spot)
        pass_on(spot, [c_dev])

    def diagonal(k):
        for h in range(2):
            spot = place(oy, ox, h, c, line[k])
            arrive(spot)
            pass_on(spot, [near, c_dev] if k == 0 else [c_dev])

    near, across = device(line[1], y, x, c), device(3 - z, y, x, c)
    for h in range(2):
        if h == 1:
            stage(1)
        spot = place(y, x, h, c, z)
        pass_on(spot, [near])
        inner_on(spot, across)
        pass_on(spot, [x_dev, y_dev, c_dev])
    for k in range(1, 4):
        for h in range(2):
            spot = place(y, x, h, c, line[k])
            arrive(spot)
            inner_on(spot, across if k == 1 else near)
            pass_on(spot, [x_dev, y_dev, c_dev])
        neighbours(k - 1)
    diagonal(0)
    w_copy.wait()
    sibling_line(y, x)
    compute(0, y, x)
    neighbours(3)
    sibling_line(y, ox)
    compute(1, y, ox)
    diagonal(2)
    sibling_line(oy, x)
    compute(2, oy, x)
    diagonal(1)
    diagonal(3)

    lo, hi = pl.ds(0, quarter), pl.ds(quarter, quarter)

    def joined(u, j, rows):
        return mine[u, j, rows] + cr[u, j, rows].astype(jnp.float32)

    def first(i, j, u, rows, dev):
        p1s[i, j] = joined(u, j, rows).astype(jnp.bfloat16)
        send(p1s.at[i, j], p1r.at[i, j], p1_sem.at[i * parts + j], dev)

    def start(j):
        landed(cr.at[3, j], c_sem.at[3 + j])
        first(2, j, 3, lo, y_dev)
        first(3, j, 3, hi, x_dev)

    for u in range(3):
        landed(cr.at[u], c_sem.at[u])
    for j in range(parts):
        first(0, j, 2, lo, y_dev)
        first(1, j, 1, hi, x_dev)
    sibling_line(oy, ox)
    compute(3, oy, ox)
    start(parts - 1)

    for j in range(parts):
        for i, u, rows, dev in ((0, 1, lo, x_dev), (1, 2, hi, y_dev)):
            landed(p1r.at[2 + i, j], p1_sem.at[(2 + i) * parts + j])
            p2s[i, j] = (joined(u, j, rows) + p1r[2 + i, j].astype(jnp.float32)).astype(jnp.bfloat16)
            send(p2s.at[i, j], p2r.at[i, j], p2_sem.at[i * parts + j], dev)
    for j in range(parts):
        for i, rows in ((0, lo), (1, hi)):
            landed(p1r.at[i, j], p1_sem.at[i * parts + j])
            tot[j, rows] = joined(0, j, rows) + p1r[i, j].astype(jnp.float32)

    def part(j, h, cc, zz):
        return tot[j, pl.ds(pl.multiple_of(((h * 2 + cc) * 4 + zz) * per, per), per)]

    for j in range(parts):
        for i, rows in ((0, lo), (1, hi)):
            landed(p2r.at[i, j], p2_sem.at[i * parts + j])
            tot[j, rows] = tot[j, rows] + p2r[i, j].astype(jnp.float32)
        for k in range(1, 4):
            for h in range(2):
                for cc in range(2):
                    at = (h * 2 + cc) * per
                    zs[k, j, at : at + per] = part(j, h, cc, others[k]).astype(jnp.bfloat16)
            send(zs.at[k, j], zr.at[k, j], z_sem.at[k * parts + j], z_dev[k])

    def final(j, h, cc):
        total = part(j, h, cc, z)
        rows = pl.ds(pl.multiple_of((h * 2 + cc) * per, per), per)
        for k in range(1, 4):
            total = total + zr[k, j, rows].astype(jnp.float32)
        return total.astype(jnp.bfloat16)

    for j in range(parts):
        for k in range(1, 4):
            landed(zr.at[k, j], z_sem.at[k * parts + j])
        for h in range(2):
            fs[j, h] = final(j, h, oc)
        send(fs.at[j], fr.at[j], f_sem.at[j], c_dev)
        for h in range(2):
            out[h, :, pl.ds(pl.multiple_of(c * half + j * 256, 256), 256)] = final(j, h, c)
    for j in range(parts):
        landed(fr.at[j], f_sem.at[j])
        for h in range(2):
            out[h, :, pl.ds(pl.multiple_of(oc * half + j * 256, 256), 256)] = fr[j, h]
    for copy in copies:
        copy.wait_send()

    @pl.when(inner)
    def _():
        for copy in inner_copies:
            copy.wait_send()


def fused(tokens, routes, gates, weights):
    n_ep = lax.axis_size("ep")
    micro, per, width = tokens.shape
    ff = weights.shape[2]
    half, quarter = ff // 2, 8 * per
    parts = half // 256
    bf, f32 = jnp.bfloat16, jnp.float32
    vmem = pl.BlockSpec(memory_space=pltpu.VMEM)
    return pl.pallas_call(
        functools.partial(kernel, per, width, ff, n_ep),
        out_shape=jax.ShapeDtypeStruct((micro, per, ff), bf),
        in_specs=[vmem, vmem, vmem, pl.BlockSpec(memory_space=pl.ANY)],
        out_specs=vmem,
        scratch_shapes=[
            pltpu.VMEM((n_ep * 2 * per, width + 128), bf),
            pltpu.VMEM((width, ff), bf),
            pltpu.VMEM((4, parts, 2 * quarter, 256), f32),
            pltpu.VMEM((4, parts, 2 * quarter, 256), bf),
            pltpu.VMEM((4, parts, 2 * quarter, 256), bf),
            pltpu.VMEM((4, parts, quarter, 256), bf),
            pltpu.VMEM((4, parts, quarter, 256), bf),
            pltpu.VMEM((2, parts, quarter, 256), bf),
            pltpu.VMEM((2, parts, quarter, 256), bf),
            pltpu.VMEM((parts, 2 * quarter, 256), f32),
            pltpu.VMEM((4, parts, 4 * per, 256), bf),
            pltpu.VMEM((4, parts, 4 * per, 256), bf),
            pltpu.VMEM((parts, 2, per, 256), bf),
            pltpu.VMEM((parts, 2, per, 256), bf),
            pltpu.SemaphoreType.DMA,
            pltpu.SemaphoreType.DMA((112,)),
            pltpu.SemaphoreType.DMA((64,)),
            pltpu.SemaphoreType.DMA((3 + parts,)),
            pltpu.SemaphoreType.DMA((4 * parts,)),
            pltpu.SemaphoreType.DMA((2 * parts,)),
            pltpu.SemaphoreType.DMA((4 * parts,)),
            pltpu.SemaphoreType.DMA((parts,)),
        ],
        compiler_params=pltpu.CompilerParams(
            collective_id=0, has_side_effects=True, vmem_limit_bytes=48 * 1024 * 1024
        ),
        cost_estimate=pl.CostEstimate(
            flops=2 * n_ep * 2 * per * width * ff,
            bytes_accessed=2 * width * ff,
            transcendentals=n_ep * 2 * per * ff,
        ),
    )(tokens, routes, gates, weights)


def restore(tokens):
    rows, width = tokens.shape
    grouped = tokens.astype(jnp.float32).reshape(rows, width // 128, 128)
    amax = jnp.max(jnp.abs(grouped), axis=2)
    scale = ((amax + 1e-06) / 448.0).astype(jnp.bfloat16).astype(jnp.float32)[:, :, None]
    quant = (grouped / scale).astype(jnp.bfloat16)
    return (quant.astype(jnp.float32) * scale).astype(jnp.bfloat16).reshape(rows, width)


def shards(tokens, routes, gates, weights):
    n_ep = lax.axis_size("ep")
    local = weights.shape[0]
    experts = local * n_ep
    micro, per, width = tokens.shape
    rows = micro * per
    restored = restore(tokens.reshape(rows, width))
    ids = routes.reshape(rows, -1)
    values = gates.reshape(rows, -1)
    names = jnp.arange(experts, dtype=jnp.int32)
    dense = jnp.sum(
        jnp.where(ids[:, :, None] == names[None, None, :], values[:, :, None], 0.0), axis=1
    )
    share = lax.all_to_all(
        dense.reshape(rows, n_ep, local), "ep", split_axis=1, concat_axis=0, tiled=True
    ).reshape(n_ep * rows, local)
    everyone = lax.all_gather(restored, "ep", axis=0, tiled=True)
    total = 0.0
    for j in range(local):
        hidden = jnp.dot(everyone, weights[j], preferred_element_type=jnp.float32)
        act = jax.nn.silu(hidden).astype(jnp.bfloat16).astype(jnp.float32)
        gate = share[:, j : j + 1]
        total = total + jnp.where(gate > 0.0, act, 0.0) * gate
    mixed = lax.psum_scatter(total, "ep", scatter_dimension=0, tiled=True)
    return mixed.astype(jnp.bfloat16).reshape(micro, per, -1)


def solution(mesh):
    placed = (
        P(None, ("replica", "ep"), None),
        P(None, ("replica", "ep"), None),
        P(None, ("replica", "ep"), None),
        P("ep", None, None),
    )
    small = mesh.shape["ep"] == 32 and mesh.shape["replica"] == 1
    return jax.shard_map(
        fused if small else shards,
        mesh=mesh,
        in_specs=placed,
        out_specs=P(None, ("replica", "ep"), None),
        check_vma=False,
    )
```

```python
import functools

import jax
import jax.numpy as jnp
from jax import lax
from jax.experimental import pallas as pl
from jax.experimental.pallas import tpu as pltpu
from jax.sharding import PartitionSpec as P


MESH = pl.DeviceIdType.MESH


def kernel(per, width, ff, experts, tok, routes, gates, w_hbm, out,
           got, w, mine, cs, cr, p1s, p1r, p2s, p2r, tot, zs, zr, fs, fr,
           w_sem, send_sem, got_sem, c_sem, p1_sem, p2_sem, z_sem, f_sem):
    me = lax.axis_index("ep")
    c, x, y, z = me % 2, (me // 2) % 2, (me // 4) % 2, me // 8
    ox, oy, oc = 1 - x, 1 - y, 1 - c
    half = ff // 2
    quarter = 8 * per
    parts = half // 256

    def device(zz, yy, xx, cc):
        return ((zz * 2 + yy) * 2 + xx) * 2 + cc

    def place(yy, xx, h, cc, zz):
        return (((yy * 2 + xx) * 2 + h) * 2 + cc) * 4 + zz

    others = [(z + k) % 4 for k in range(4)]
    far = z // 2
    line = [z, z + 1 - 2 * (z % 2), 2 - far, 3 - 3 * far]
    inner = (z == 1) | (z == 2)
    x_dev, y_dev, c_dev = device(z, y, ox, c), device(z, oy, x, c), device(z, y, x, oc)
    z_dev = [device(others[k], y, x, c) for k in range(4)]

    w_copy = pltpu.make_async_copy(w_hbm.at[0], w, w_sem)
    w_copy.start()
    barrier = pltpu.get_barrier_semaphore()
    for dev in (x_dev, y_dev, c_dev, z_dev[1], z_dev[2], z_dev[3]):
        pl.semaphore_signal(barrier, inc=1, device_id={"ep": dev}, device_id_type=MESH)

    lane = lax.broadcasted_iota(jnp.int32, (per, 128), 1)

    def stage(h):
        rows = pl.ds(pl.multiple_of(place(y, x, h, c, z) * per, per), per)
        for g in range(width // 128):
            v = tok[h, :, g * 128 : (g + 1) * 128].astype(jnp.float32)
            amax = jnp.max(jnp.abs(v), axis=1, keepdims=True)
            scale = ((amax + 1e-06) / 448.0).astype(jnp.bfloat16).astype(jnp.float32)
            quant = (v / scale).astype(jnp.bfloat16).astype(jnp.float32)
            got[rows, g * 128 : (g + 1) * 128] = (quant * scale).astype(jnp.bfloat16)
        names, values = routes[h], gates[h]
        high = jnp.zeros((per, 128), jnp.float32)
        low = jnp.zeros((per, 128), jnp.float32)
        for k in range(names.shape[1]):
            name, value = names[:, k : k + 1], values[:, k : k + 1]
            high = high + jnp.where(lane == name, value, 0.0)
            low = low + jnp.where(lane - experts == name, value, 0.0)
        low = low - low.astype(jnp.bfloat16).astype(jnp.float32)
        got[rows, width : width + 128] = jnp.where(lane < experts, high, low).astype(jnp.bfloat16)

    stage(0)
    pl.semaphore_wait(barrier, 6)

    copies, inner_copies = [], []

    def prepare(src, dst, sem, dev):
        return pltpu.make_async_remote_copy(
            src_ref=src, dst_ref=dst, send_sem=send_sem.at[len(copies) + len(inner_copies)],
            recv_sem=sem, device_id={"ep": dev}, device_id_type=MESH,
        )

    def send(src, dst, sem, dev):
        copy = prepare(src, dst, sem, dev)
        copy.start()
        copies.append(copy)

    def inner_on(spot, dev):
        copy = prepare(block(spot), block(spot), got_sem.at[spot], dev)
        inner_copies.append(copy)

        @pl.when(inner)
        def _():
            copy.start()

    def landed(dst, sem):
        pltpu.make_async_remote_copy(
            src_ref=dst, dst_ref=dst, send_sem=send_sem.at[0], recv_sem=sem,
            device_id={"ep": c_dev}, device_id_type=MESH,
        ).wait_recv()

    def block(spot):
        return got.at[pl.ds(pl.multiple_of(spot * per, per), per)]

    def pass_on(spot, devs):
        for dev in devs:
            send(block(spot), block(spot), got_sem.at[spot], dev)

    def arrive(spot):
        landed(block(spot), got_sem.at[spot])

    def sibling_line(yy, xx):
        for h in range(2):
            for k in range(4):
                arrive(place(yy, xx, h, oc, line[k]))

    def compute(u, yy, xx):
        base = place(yy, xx, 0, 0, 0) * per
        rows = pl.ds(pl.multiple_of(base, 2 * quarter), 2 * quarter)
        wide = lax.broadcasted_iota(jnp.int32, (2 * quarter, 128), 1)
        share = got[rows, width : width + 128].astype(jnp.float32)
        picked = (wide == me) | (wide == me + experts)
        gate = jnp.sum(jnp.where(picked, share, 0.0), axis=1, keepdims=True)

        def tile(col):
            cols = pl.ds(pl.multiple_of(col, 256), 256)
            v = jnp.dot(got[rows, :width], w[:, cols], preferred_element_type=jnp.float32)
            return (gate * (0.5 * v)) * (1.0 + jnp.tanh(0.5 * v))

        for j in range(parts):
            cs[u, j] = tile(oc * half + j * 256).astype(jnp.bfloat16)
            if u == 3:
                send(cs.at[u, j], cr.at[u, j], c_sem.at[u + j], c_dev)
                mine[u, j] = tile(c * half + j * 256)
                if j > 0:
                    start(j - 1)
        if u < 3:
            send(cs.at[u], cr.at[u], c_sem.at[u], c_dev)
            for j in range(parts):
                mine[u, j] = tile(c * half + j * 256)

    def neighbours(k):
        spot = place(y, ox, 0, c, line[k])
        arrive(spot)
        pass_on(spot, [c_dev] if k == 1 else [y_dev, c_dev])
        spot = place(oy, x, 1, c, line[k])
        arrive(spot)
        pass_on(spot, [c_dev] if k == 1 else [x_dev, c_dev])
        spot = place(y, ox, 1, c, line[k])
        arrive(spot)
        pass_on(spot, [c_dev])
        spot = place(oy, x, 0, c, line[k])
        arrive(spot)
        pass_on(spot, [c_dev])

    def diagonal(k):
        for h in range(2):
            spot = place(oy, ox, h, c, line[k])
            arrive(spot)
            pass_on(spot, [near, c_dev] if k == 0 else [c_dev])

    near, across = device(line[1], y, x, c), device(3 - z, y, x, c)
    for h in range(2):
        if h == 1:
            stage(1)
        spot = place(y, x, h, c, z)
        pass_on(spot, [near])
        inner_on(spot, across)
        pass_on(spot, [x_dev, y_dev, c_dev])
    for k in range(1, 4):
        for h in range(2):
            spot = place(y, x, h, c, line[k])
            arrive(spot)
            inner_on(spot, across if k == 1 else near)
            pass_on(spot, [x_dev, y_dev, c_dev])
        neighbours(k - 1)
    diagonal(0)
    w_copy.wait()
    sibling_line(y, x)
    compute(0, y, x)
    neighbours(3)
    sibling_line(y, ox)
    compute(1, y, ox)
    diagonal(2)
    sibling_line(oy, x)
    compute(2, oy, x)
    diagonal(1)
    diagonal(3)

    lo, hi = pl.ds(0, quarter), pl.ds(quarter, quarter)

    def joined(u, j, rows):
        return mine[u, j, rows] + cr[u, j, rows].astype(jnp.float32)

    def first(i, j, u, rows, dev):
        p1s[i, j] = joined(u, j, rows).astype(jnp.bfloat16)
        send(p1s.at[i, j], p1r.at[i, j], p1_sem.at[i * parts + j], dev)

    def start(j):
        landed(cr.at[3, j], c_sem.at[3 + j])
        first(2, j, 3, lo, y_dev)
        first(3, j, 3, hi, x_dev)

    for u in range(3):
        landed(cr.at[u], c_sem.at[u])
    for j in range(parts):
        first(0, j, 2, lo, y_dev)
        first(1, j, 1, hi, x_dev)
    sibling_line(oy, ox)
    compute(3, oy, ox)
    start(parts - 1)

    for j in range(parts):
        for i, u, rows, dev in ((0, 1, lo, x_dev), (1, 2, hi, y_dev)):
            landed(p1r.at[2 + i, j], p1_sem.at[(2 + i) * parts + j])
            p2s[i, j] = (joined(u, j, rows) + p1r[2 + i, j].astype(jnp.float32)).astype(jnp.bfloat16)
            send(p2s.at[i, j], p2r.at[i, j], p2_sem.at[i * parts + j], dev)
    for j in range(parts):
        for i, rows in ((0, lo), (1, hi)):
            landed(p1r.at[i, j], p1_sem.at[i * parts + j])
            tot[j, rows] = joined(0, j, rows) + p1r[i, j].astype(jnp.float32)

    def part(j, h, cc, zz):
        return tot[j, pl.ds(pl.multiple_of(((h * 2 + cc) * 4 + zz) * per, per), per)]

    for j in range(parts):
        for i, rows in ((0, lo), (1, hi)):
            landed(p2r.at[i, j], p2_sem.at[i * parts + j])
            tot[j, rows] = tot[j, rows] + p2r[i, j].astype(jnp.float32)
        for k in (2, 1, 3):
            for h in range(2):
                for cc in range(2):
                    at = (h * 2 + cc) * per
                    zs[k, j, at : at + per] = part(j, h, cc, others[k]).astype(jnp.bfloat16)
            send(zs.at[k, j], zr.at[k, j], z_sem.at[k * parts + j], z_dev[k])

    def final(j, h, cc):
        total = part(j, h, cc, z)
        rows = pl.ds(pl.multiple_of((h * 2 + cc) * per, per), per)
        for k in range(1, 4):
            total = total + zr[k, j, rows].astype(jnp.float32)
        return total.astype(jnp.bfloat16)

    for j in range(parts):
        for k in range(1, 4):
            landed(zr.at[k, j], z_sem.at[k * parts + j])
        for h in range(2):
            fs[j, h] = final(j, h, oc)
        send(fs.at[j], fr.at[j], f_sem.at[j], c_dev)
        for h in range(2):
            out[h, :, pl.ds(pl.multiple_of(c * half + j * 256, 256), 256)] = final(j, h, c)
    for j in range(parts):
        landed(fr.at[j], f_sem.at[j])
        for h in range(2):
            out[h, :, pl.ds(pl.multiple_of(oc * half + j * 256, 256), 256)] = fr[j, h]
    for copy in copies:
        copy.wait_send()

    @pl.when(inner)
    def _():
        for copy in inner_copies:
            copy.wait_send()


def fused(tokens, routes, gates, weights):
    n_ep = lax.axis_size("ep")
    micro, per, width = tokens.shape
    ff = weights.shape[2]
    half, quarter = ff // 2, 8 * per
    parts = half // 256
    bf, f32 = jnp.bfloat16, jnp.float32
    vmem = pl.BlockSpec(memory_space=pltpu.VMEM)
    return pl.pallas_call(
        functools.partial(kernel, per, width, ff, n_ep),
        out_shape=jax.ShapeDtypeStruct((micro, per, ff), bf),
        in_specs=[vmem, vmem, vmem, pl.BlockSpec(memory_space=pl.ANY)],
        out_specs=vmem,
        scratch_shapes=[
            pltpu.VMEM((n_ep * 2 * per, width + 128), bf),
            pltpu.VMEM((width, ff), bf),
            pltpu.VMEM((4, parts, 2 * quarter, 256), f32),
            pltpu.VMEM((4, parts, 2 * quarter, 256), bf),
            pltpu.VMEM((4, parts, 2 * quarter, 256), bf),
            pltpu.VMEM((4, parts, quarter, 256), bf),
            pltpu.VMEM((4, parts, quarter, 256), bf),
            pltpu.VMEM((2, parts, quarter, 256), bf),
            pltpu.VMEM((2, parts, quarter, 256), bf),
            pltpu.VMEM((parts, 2 * quarter, 256), f32),
            pltpu.VMEM((4, parts, 4 * per, 256), bf),
            pltpu.VMEM((4, parts, 4 * per, 256), bf),
            pltpu.VMEM((parts, 2, per, 256), bf),
            pltpu.VMEM((parts, 2, per, 256), bf),
            pltpu.SemaphoreType.DMA,
            pltpu.SemaphoreType.DMA((112,)),
            pltpu.SemaphoreType.DMA((64,)),
            pltpu.SemaphoreType.DMA((3 + parts,)),
            pltpu.SemaphoreType.DMA((4 * parts,)),
            pltpu.SemaphoreType.DMA((2 * parts,)),
            pltpu.SemaphoreType.DMA((4 * parts,)),
            pltpu.SemaphoreType.DMA((parts,)),
        ],
        compiler_params=pltpu.CompilerParams(
            collective_id=0, has_side_effects=True, vmem_limit_bytes=48 * 1024 * 1024
        ),
        cost_estimate=pl.CostEstimate(
            flops=2 * n_ep * 2 * per * width * ff,
            bytes_accessed=2 * width * ff,
            transcendentals=n_ep * 2 * per * ff,
        ),
    )(tokens, routes, gates, weights)


def restore(tokens):
    rows, width = tokens.shape
    grouped = tokens.astype(jnp.float32).reshape(rows, width // 128, 128)
    amax = jnp.max(jnp.abs(grouped), axis=2)
    scale = ((amax + 1e-06) / 448.0).astype(jnp.bfloat16).astype(jnp.float32)[:, :, None]
    quant = (grouped / scale).astype(jnp.bfloat16)
    return (quant.astype(jnp.float32) * scale).astype(jnp.bfloat16).reshape(rows, width)


def shards(tokens, routes, gates, weights):
    n_ep = lax.axis_size("ep")
    local = weights.shape[0]
    experts = local * n_ep
    micro, per, width = tokens.shape
    rows = micro * per
    restored = restore(tokens.reshape(rows, width))
    ids = routes.reshape(rows, -1)
    values = gates.reshape(rows, -1)
    names = jnp.arange(experts, dtype=jnp.int32)
    dense = jnp.sum(
        jnp.where(ids[:, :, None] == names[None, None, :], values[:, :, None], 0.0), axis=1
    )
    share = lax.all_to_all(
        dense.reshape(rows, n_ep, local), "ep", split_axis=1, concat_axis=0, tiled=True
    ).reshape(n_ep * rows, local)
    everyone = lax.all_gather(restored, "ep", axis=0, tiled=True)
    total = 0.0
    for j in range(local):
        hidden = jnp.dot(everyone, weights[j], preferred_element_type=jnp.float32)
        act = jax.nn.silu(hidden).astype(jnp.bfloat16).astype(jnp.float32)
        gate = share[:, j : j + 1]
        total = total + jnp.where(gate > 0.0, act, 0.0) * gate
    mixed = lax.psum_scatter(total, "ep", scatter_dimension=0, tiled=True)
    return mixed.astype(jnp.bfloat16).reshape(micro, per, -1)


def solution(mesh):
    placed = (
        P(None, ("replica", "ep"), None),
        P(None, ("replica", "ep"), None),
        P(None, ("replica", "ep"), None),
        P("ep", None, None),
    )
    small = mesh.shape["ep"] == 32 and mesh.shape["replica"] == 1
    return jax.shard_map(
        fused if small else shards,
        mesh=mesh,
        in_specs=placed,
        out_specs=P(None, ("replica", "ep"), None),
        check_vma=False,
    )
```
